32 devices in a mesh: dp: 4 (over y, core), row: 2 (over x), col: 4 (over z).
Axes of the slice: x: 2, y: 2, z: 4, core: 2. Of those that a mesh axis runs over, the one named last changes fastest.
Arguments:
- inputs: bfloat16 [6144, 1024], P(('dp', 'row'), 'col'), may hold values from -14 to 14
- cotangent: bfloat16 [6144, 1024], P(('dp', 'row'), 'col'), may hold values from -20 to 20
- routes: int32 [6144, 8], P('dp'), may hold values from 0 to 31, all different within a row; in each aligned block of 1536 rows (0 to 1535, 1536 to 3071, ...) at most 480 rows name the same one
- gate_probs: float32 [6144, 8], P('dp'), may hold values from 0.06 to 0.2
- seq_ids: int32 [6144], P('dp'), may hold values from 0 to 2, as said below
- norm_gains: float32 [2, 1024], P(None, 'col'), may hold values from 0.5 to 1.5
- gain_moment: float32 [2, 1024], P(None, 'col'), may hold values from -112 to 112
- gain_second: float32 [2, 1024], P(None, 'col'), may hold values from 1290.24 to 5160.96
- query_weight: float32 [1024, 1024], P('col', 'row'), may hold values from -0.1875 to 0.1875
- query_moment: float32 [1024, 1024], P('col', 'row'), may hold values from -112 to 112
- query_second: float32 [1024, 1024], P('col', 'row'), may hold values from 1300.48 to 5222.4
- key_value_matrix: float32 [2, 1024, 512], P(None, 'col', 'row'), may hold values from -0.1875 to 0.1875
- key_value_first_moment: float32 [2, 1024, 512], P(None, 'col', 'row'), may hold values from -112 to 112
- key_value_second_moment: float32 [2, 1024, 512], P(None, 'col', 'row'), may hold values from 1300.48 to 5222.4
- out_weight: float32 [1024, 1024], P('row', 'col'), may hold values from -3 to 3
- out_moment: float32 [1024, 1024], P('row', 'col'), may hold values from -7 to 7
- out_second: float32 [1024, 1024], P('row', 'col'), may hold values from 5.08 to 20.4
- gate_up_weight: float32 [32, 1024, 2, 512], P('dp', 'col', None, 'row'), may hold values from -0.1875 to 0.1875
- gate_up_moment: float32 [32, 1024, 2, 512], P('dp', 'col', None, 'row'), may hold values from -20 to 20
- gate_up_second: float32 [32, 1024, 2, 512], P('dp', 'col', None, 'row'), may hold values from 50.9952 to 202.752
- down_weight: float32 [32, 512, 1024], P('dp', 'row', 'col'), may hold values from -1 to 1
- down_moment: float32 [32, 512, 1024], P('dp', 'row', 'col'), may hold values from -4 to 4
- down_second: float32 [32, 512, 1024], P('dp', 'row', 'col'), may hold values from 2.08896 to 8.2944
Outputs:
- block_output: bfloat16 [6144, 1024], P(('dp', 'row'), 'col')
- input_grad: float32 [6144, 1024], P(('dp', 'row'), 'col')
- gain_moment_new: float32 [2, 1024], P(None, 'col')
- gain_second_new: float32 [2, 1024], P(None, 'col')
- gains_new: float32 [2, 1024], P(None, 'col')
- query_moment_new: float32 [1024, 1024], P('col', 'row')
- query_second_new: float32 [1024, 1024], P('col', 'row')
- query_new: float32 [1024, 1024], P('col', 'row')
- key_value_moment_new: float32 [2, 1024, 512], P(None, 'col', 'row')
- key_value_second_new: float32 [2, 1024, 512], P(None, 'col', 'row')
- key_value_new: float32 [2, 1024, 512], P(None, 'col', 'row')
- out_moment_new: float32 [1024, 1024], P('row', 'col')
- out_second_new: float32 [1024, 1024], P('row', 'col')
- out_new: float32 [1024, 1024], P('row', 'col')
- gate_up_moment_new: float32 [32, 1024, 2, 512], P('dp', 'col', None, 'row')
- gate_up_second_new: float32 [32, 1024, 2, 512], P('dp', 'col', None, 'row')
- gate_up_new: float32 [32, 1024, 2, 512], P('dp', 'col', None, 'row')
- down_moment_new: float32 [32, 512, 1024], P('dp', 'row', 'col')
- down_second_new: float32 [32, 512, 1024], P('dp', 'row', 'col')
- down_new: float32 [32, 512, 1024], P('dp', 'row', 'col')
The draws below stay inside these ranges and needn't reach their ends.
Inputs may be any that keep to these rules, and one draw needn't show every extreme that they name: `routes`: each row names 8 different experts; in each aligned block of 1536 rows (one replica) no expert is named by more than 480 rows, a bound that some block reaches. `seq_ids`: in each aligned block of 1536 tokens the numbers never fall, start at 0 and end at 2; sequence 1 begins within the block's first quarter and ends within its last quarter.
All inputs are finite; a program needn't handle non-finite values.
Results may differ from the reference program's by a relative error of at most 0.013.
The reference program's roundings to bfloat16 on the way count: a program that leaves them out, or rounds other values in their place, can miss the bound.
Values may be sent and summed in bfloat16 or wider, within the bound.
A program may use at most 256 MiB of HBM per device.

```python
import math
import jax
import jax.numpy as jnp
import numpy as np
from jax import lax

MODEL_WIDTH = 1024
QUERY_HEADS = 16
KEY_VALUE_HEADS = 8
HEAD_SIZE = 64
FF = 512
EXPERTS = 32
TOP = 8
STEP = 10
REPLICA_TOKENS = 1536
TOKEN_TOTAL = 6144
CAP = 480
N_DP = 4
N_COL = 4


def draw_inputs(key, part):
    key = jax.random.fold_in(key, 1)
    noise_key, column_key = jax.random.split(key)
    columns = jnp.arange(MODEL_WIDTH, dtype=jnp.float32) / MODEL_WIDTH
    spread = jnp.exp(jax.random.uniform(column_key, (MODEL_WIDTH,), jnp.float32, -0.7, 0.7))
    value_rows = jnp.clip(jax.random.normal(noise_key, (TOKEN_TOTAL, MODEL_WIDTH), jnp.float32), -4.0, 4.0)
    trend = jnp.sqrt(1.0 + 2.0 * columns)
    return (value_rows * trend[None, :] * spread[None, :]).astype(jnp.bfloat16)


def draw_cotangent(key, part):
    key = jax.random.fold_in(key, 2)
    placed = jnp.arange(TOKEN_TOTAL, dtype=jnp.float32)[:, None] / TOKEN_TOTAL
    value_rows = jnp.clip(jax.random.normal(key, (TOKEN_TOTAL, MODEL_WIDTH), jnp.float32), -4.0, 4.0)
    trend = 1.0 + 2.0 * placed
    return (value_rows * trend).astype(jnp.bfloat16)


def draw_seq_ids(key, part):
    key = jax.random.fold_in(key, 3)
    replicas = TOKEN_TOTAL // REPLICA_TOKENS
    quarter = REPLICA_TOKENS // 4
    first_key, last_key = jax.random.split(key)
    starts = jax.random.randint(first_key, (replicas, 1), 1, quarter)
    finish = jax.random.randint(last_key, (replicas, 1), REPLICA_TOKENS - quarter + 1, REPLICA_TOKENS)
    positions = jnp.arange(REPLICA_TOKENS, dtype=jnp.int32)[None, :]
    numbers = (positions >= starts).astype(jnp.int32) + (positions >= finish).astype(jnp.int32)
    return numbers.reshape(TOKEN_TOTAL).astype(jnp.int32)


def level_of(rng, shape, cuts, least, top_value):
    gain, own = 1.0, jax.random.fold_in(rng, 6)
    for dim, shards_of in cuts:
        draws = jnp.exp(jax.random.uniform(jax.random.fold_in(own, dim), (shards_of,), jnp.float32, least / len(cuts), top_value / len(cuts)))
        gain = gain * jnp.repeat(draws, shape[dim] // shards_of).reshape([-1 if axis == dim else 1 for axis in range(len(shape))])
    return gain


def routed_block(own_key, own, number, rows, number_of, top, bound, lean):
    order = jax.random.permutation(own_key, number_of)
    crowded, ordinary = shares(number_of, rows * top, bound, lean, True), shares(number_of, rows * top, bound, lean, False)
    places = jnp.arange(number_of)

    def named(sizes, rotation):
        used = int((sizes > 0).sum())
        fixed = max(1, used // 4)
        passed = fixed + (places - fixed + rotation * (used - fixed)) % max(1, number_of - fixed)
        return jnp.zeros((number_of,), jnp.int32).at[order[jnp.where(places < fixed, places, passed)]].set(jnp.asarray(sizes, jnp.int32))

    sizes = jnp.where(number % 4 == 0, named(crowded, number // 4), named(ordinary, number - number // 4 - 1))
    mixed = jax.random.permutation(jax.random.fold_in(own, 3), number_of)
    giver, sink = mixed[0:number_of // 2 * 2:2], mixed[1:number_of // 2 * 2:2]
    slack = jnp.minimum(sizes[giver] - 1, bound - sizes[sink]) // 2
    slack = jnp.where((giver == order[0]) | (sink == order[0]) | (sizes[sink] == 0), 0, jnp.maximum(slack, 0))
    passed = jax.random.randint(jax.random.fold_in(own, 4), (number_of // 2,), 0, 1 << 20) % (slack + 1)
    sizes = sizes.at[giver].add(-passed).at[sink].add(passed)
    labels = jnp.searchsorted(jnp.cumsum(sizes), jnp.arange(rows * top), side="right").astype(jnp.int32)
    listing = labels.reshape(top, rows).T
    listing = listing[jax.random.permutation(jax.random.fold_in(own, 1), rows)]
    rotation = jax.random.randint(jax.random.fold_in(own, 2), (rows, 1), 0, top)
    return jnp.take_along_axis(listing, (jnp.arange(top)[None, :] + rotation) % top, axis=1)


def shares(count, total, bound, slope, full):
    loads = [(1 << 20) // math.isqrt(rank ** slope) + 1 for rank in range(1, count + 1)]
    largest = bound if full else min(bound, max(-(-total // count), total * loads[0] // sum(loads)))
    least = 1 if total - largest >= count - 1 else 0
    holding, rest = [largest] + [least] * (count - 1), total - largest - least * (count - 1)
    while rest > 0:
        movable = [i for i in range(1, count) if holding[i] < largest] or [i for i in range(1, count) if holding[i] < bound]
        mass, budget = sum([loads[i] for i in movable]), rest
        for i in movable:
            extra = min(bound - holding[i], max(1, budget * loads[i] // mass), rest)
            holding[i] = holding[i] + extra
            rest = rest - extra
    return np.array(holding)


def noise(key, extent, width, limit, pieces=(), held_as=jnp.bfloat16):
    gain = level_of(key, extent, pieces, -0.22, 0.18) if pieces else 1.0
    drawn = jax.random.normal(key, extent, jnp.float32) * width * gain
    return jnp.minimum(jnp.maximum(drawn, -limit), limit).astype(held_as)


def setup_inputs(seed: int = 0) -> dict:
    streams_of = jax.random.split(jax.random.key(seed), 24)
    inputs = draw_inputs(jax.random.fold_in(streams_of[23], 71), 0)
    cotangent = draw_cotangent(jax.random.fold_in(streams_of[23], 71), 0)
    routes_keys = jax.random.split(jax.random.fold_in(streams_of[2], 1), TOKEN_TOTAL // REPLICA_TOKENS)
    routes_turns = jax.random.permutation(jax.random.fold_in(streams_of[2], 3), TOKEN_TOTAL // REPLICA_TOKENS)
    routes = jax.vmap(lambda own, number: routed_block(jax.random.fold_in(streams_of[2], 2), own, number, REPLICA_TOKENS, EXPERTS, TOP, CAP, 1))(routes_keys, routes_turns).reshape((TOKEN_TOTAL, TOP))
    gate_probs = jnp.clip(0.06 + 0.14 * jax.random.uniform(streams_of[3], (TOKEN_TOTAL, TOP), jnp.float32) ** level_of(streams_of[3], (TOKEN_TOTAL, TOP), ((0, 4),), -0.2, 0.2), 0.06, 0.2)
    seq_ids = draw_seq_ids(jax.random.fold_in(streams_of[23], 71), 0)
    norm_gains = jnp.clip(1.0 + 0.1 * jax.random.normal(streams_of[5], (2, MODEL_WIDTH), jnp.float32), 0.5, 1.5)
    gain_moment = noise(streams_of[6], (2, MODEL_WIDTH), (0.22 * TOKEN_TOTAL ** 0.5), 112.0, ((1, 4),), jnp.float32)
    gain_second = jnp.clip(jnp.exp(math.log(5160.96) - 1.3862944 * jax.random.uniform(streams_of[7], (2, MODEL_WIDTH), jnp.float32) ** level_of(streams_of[7], (2, MODEL_WIDTH), ((1, 4),), -0.2, 0.2)), 1290.24, 5160.96)
    query_weight = noise(streams_of[8], (MODEL_WIDTH, QUERY_HEADS * HEAD_SIZE), MODEL_WIDTH ** -0.5, 0.1875, ((0, 4), (1, 2)), jnp.float32)
    query_moment = noise(streams_of[9], (MODEL_WIDTH, QUERY_HEADS * HEAD_SIZE), (0.22 * (6 * (MODEL_WIDTH // max(1, QUERY_HEADS * HEAD_SIZE // 256)) * (TOKEN_TOTAL // REPLICA_TOKENS)) ** 0.5), 112.0, ((0, 4), (1, 2)), jnp.float32)
    query_second = jnp.clip(jnp.exp(math.log(5222.4) - 1.3902236 * jax.random.uniform(streams_of[10], (MODEL_WIDTH, QUERY_HEADS * HEAD_SIZE), jnp.float32) ** level_of(streams_of[10], (MODEL_WIDTH, QUERY_HEADS * HEAD_SIZE), ((0, 4), (1, 2)), -0.2, 0.2)), 1300.48, 5222.4)
    key_value_matrix = noise(streams_of[11], (2, MODEL_WIDTH, KEY_VALUE_HEADS * HEAD_SIZE), MODEL_WIDTH ** -0.5, 0.1875, ((1, 4), (2, 2)), jnp.float32)
    key_value_first_moment = noise(streams_of[12], (2, MODEL_WIDTH, KEY_VALUE_HEADS * HEAD_SIZE), (0.22 * (6 * (MODEL_WIDTH // max(1, QUERY_HEADS * HEAD_SIZE // 256)) * (TOKEN_TOTAL // REPLICA_TOKENS)) ** 0.5), 112.0, ((1, 4), (2, 2)), jnp.float32)
    key_value_second_moment = jnp.clip(jnp.exp(math.log(5222.4) - 1.3902236 * jax.random.uniform(streams_of[13], (2, MODEL_WIDTH, KEY_VALUE_HEADS * HEAD_SIZE), jnp.float32) ** level_of(streams_of[13], (2, MODEL_WIDTH, KEY_VALUE_HEADS * HEAD_SIZE), ((1, 4), (2, 2)), -0.2, 0.2)), 1300.48, 5222.4)
    out_weight = noise(streams_of[14], (QUERY_HEADS * HEAD_SIZE, MODEL_WIDTH), (max(1, QUERY_HEADS * HEAD_SIZE // 256)) ** -0.5, 3.0, ((0, 2), (1, 4)), jnp.float32)
    out_moment = noise(streams_of[15], (QUERY_HEADS * HEAD_SIZE, MODEL_WIDTH), (0.22 * (6 * (TOKEN_TOTAL // REPLICA_TOKENS)) ** 0.5), 7.0, ((0, 2), (1, 4)), jnp.float32)
    out_second = jnp.clip(jnp.exp(math.log(20.4) - 1.3902236 * jax.random.uniform(streams_of[16], (QUERY_HEADS * HEAD_SIZE, MODEL_WIDTH), jnp.float32) ** level_of(streams_of[16], (QUERY_HEADS * HEAD_SIZE, MODEL_WIDTH), ((0, 2), (1, 4)), -0.2, 0.2)), 5.08, 20.4)
    gate_up_weight = noise(streams_of[17], (EXPERTS, MODEL_WIDTH, 2, FF), MODEL_WIDTH ** -0.5, 0.1875, ((0, 4), (1, 4), (3, 2)), jnp.float32)
    gate_up_moment = noise(streams_of[18], (EXPERTS, MODEL_WIDTH, 2, FF), (0.0154 * (16 * (MODEL_WIDTH // FF) * (TOKEN_TOTAL * TOP // EXPERTS)) ** 0.5), 20.0, ((0, 4), (1, 4), (3, 2)), jnp.float32)
    gate_up_second = jnp.clip(jnp.exp(math.log(202.752) - 1.380252 * jax.random.uniform(streams_of[19], (EXPERTS, MODEL_WIDTH, 2, FF), jnp.float32) ** level_of(streams_of[19], (EXPERTS, MODEL_WIDTH, 2, FF), ((0, 4), (1, 4), (3, 2)), -0.2, 0.2)), 50.9952, 202.752)
    down_weight = noise(streams_of[20], (EXPERTS, FF, MODEL_WIDTH), (FF // 16) ** -0.5, 1.0, ((0, 4), (1, 2), (2, 4)), jnp.float32)
    down_moment = noise(streams_of[21], (EXPERTS, FF, MODEL_WIDTH), (0.0176 * (TOKEN_TOTAL * TOP // EXPERTS) ** 0.5), 4.0, ((0, 4), (1, 2), (2, 4)), jnp.float32)
    down_second = jnp.clip(jnp.exp(math.log(8.2944) - 1.3789143 * jax.random.uniform(streams_of[22], (EXPERTS, FF, MODEL_WIDTH), jnp.float32) ** level_of(streams_of[22], (EXPERTS, FF, MODEL_WIDTH), ((0, 4), (1, 2), (2, 4)), -0.2, 0.2)), 2.08896, 8.2944)
    return dict(inputs=inputs, cotangent=cotangent, routes=routes, gate_probs=gate_probs, seq_ids=seq_ids, norm_gains=norm_gains, gain_moment=gain_moment, gain_second=gain_second, query_weight=query_weight, query_moment=query_moment, query_second=query_second, key_value_matrix=key_value_matrix, key_value_first_moment=key_value_first_moment, key_value_second_moment=key_value_second_moment, out_weight=out_weight, out_moment=out_moment, out_second=out_second, gate_up_weight=gate_up_weight, gate_up_moment=gate_up_moment, gate_up_second=gate_up_second, down_weight=down_weight, down_moment=down_moment, down_second=down_second)


@jax.custom_vjp
def low(v):
    return lax.optimization_barrier(v.astype(jnp.bfloat16)).astype(jnp.float32)

@jax.custom_vjp
def low_back(v):
    return v

def low_keep(v):
    return (low(v), None)

def low_pass(kept, grad):
    return (grad,)

def back_keep(v):
    return (v, None)

def back_low(kept, grad):
    return (low(grad),)
low.defvjp(low_keep, low_pass)
low_back.defvjp(back_keep, back_low)
norm_epsilon = 1e-06
first_decay = 0.9
second_decay = 0.95
adam_epsilon = 1e-08
weight_decay = 0.1
masked_score = -1e+30

def highest(formula, left, right):
    return jnp.einsum(formula, left, right, precision=lax.Precision.HIGHEST, preferred_element_type=jnp.float32)

def dispatch(route_rows, prob_rows):
    flat_routes = route_rows.reshape(-1)
    entries = flat_routes.shape[0]
    sorted_order = jnp.argsort(flat_routes, stable=True).astype(jnp.int32)
    expert_ids = jnp.arange(EXPERTS, dtype=jnp.int32)
    counts = lax.optimization_barrier(jnp.sum((flat_routes[:, None] == expert_ids[None, :]).astype(jnp.int32), axis=0))
    offsets = jnp.cumsum(counts) - counts
    slot_index = jnp.arange(CAP, dtype=jnp.int32)[:, None]
    position = jnp.minimum(offsets[None, :] + slot_index, entries - 1)
    source = sorted_order[position]
    filled = slot_index < counts[None, :]
    tokens = jnp.where(filled, source // TOP, REPLICA_TOKENS).astype(jnp.int32)
    weights = jnp.where(filled, prob_rows.reshape(-1)[source], 0.0)
    return (tokens, weights)

def attend(query_rows, key_rows, value_rows, seq_rows):
    block_row_span = REPLICA_TOKENS // N_COL
    group_width = QUERY_HEADS // KEY_VALUE_HEADS
    scale_factor = HEAD_SIZE ** (-0.5)
    positions = jnp.arange(REPLICA_TOKENS, dtype=jnp.int32)
    key_head_split = key_rows.reshape(REPLICA_TOKENS, KEY_VALUE_HEADS, HEAD_SIZE)
    value_head_split = value_rows.reshape(REPLICA_TOKENS, KEY_VALUE_HEADS, HEAD_SIZE)
    query_block_split = query_rows.reshape(N_COL, block_row_span, KEY_VALUE_HEADS, group_width, HEAD_SIZE)
    position_blocks = positions.reshape(N_COL, block_row_span)

    @jax.checkpoint
    def one_block(block_items):
        block_query, block_positions = block_items
        scores = low_back(highest('qkgd,tkd->kgqt', block_query, key_head_split) * scale_factor)
        allowed = (seq_rows[block_positions][:, None] == seq_rows[None, :]) & (positions[None, :] <= block_positions[:, None])
        scores = jnp.where(allowed[None, None], scores, masked_score)
        row_max = lax.optimization_barrier(jnp.max(scores, axis=-1, keepdims=True))
        log_total = row_max + jnp.log(lax.optimization_barrier(jnp.sum(jnp.exp(scores - row_max), axis=-1, keepdims=True)))
        prob_low = low(jnp.exp(scores - log_total))
        return highest('kgqt,tkd->qkgd', prob_low, value_head_split).reshape(block_row_span, QUERY_HEADS * HEAD_SIZE)
    return lax.map(one_block, (query_block_split, position_blocks)).reshape(REPLICA_TOKENS, QUERY_HEADS * HEAD_SIZE)

def forward(params, inputs, route_rows, prob_rows, seq_rows):
    norm_gains, query_weight, key_value_matrix, out_weight, gate_up_weight, down_weight = params
    query_low = low(query_weight)
    key_value_low = low(key_value_matrix)
    out_low = low(out_weight)
    gate_up_low = low(gate_up_weight)
    down_low = low(down_weight)
    first_scale = lax.rsqrt(lax.optimization_barrier(jnp.mean(inputs * inputs, axis=1, keepdims=True)) + norm_epsilon)
    normed = low(inputs * first_scale * norm_gains[0])
    query_rows = low(low_back(highest('td,df->tf', normed, query_low)))
    key_rows = low(low_back(highest('td,df->tf', normed, key_value_low[0])))
    value_rows = low(low_back(highest('td,df->tf', normed, key_value_low[1])))
    context = low(low_back(attend(query_rows, key_rows, value_rows, seq_rows)))
    attended = low_back(highest('tf,fd->td', context, out_low))
    middle = inputs + attended
    second_scale = lax.rsqrt(lax.optimization_barrier(jnp.mean(middle * middle, axis=1, keepdims=True)) + norm_epsilon)
    normed_two = low(middle * second_scale * norm_gains[1])
    slot_tokens, slot_weights = dispatch(route_rows, prob_rows)
    padded = jnp.concatenate([normed_two, jnp.zeros((1, MODEL_WIDTH), jnp.float32)], axis=0)
    slot_inputs = padded[slot_tokens]
    gate_up = low_back(highest('ced,edkf->cekf', slot_inputs, gate_up_low))
    hidden = low(jax.nn.silu(gate_up[:, :, 0]) * gate_up[:, :, 1])
    expert_out = low_back(highest('cef,efd->ced', hidden, down_low))
    weighted = (expert_out * slot_weights[:, :, None]).reshape(CAP * EXPERTS, MODEL_WIDTH)
    mixture = jax.ops.segment_sum(weighted, slot_tokens.reshape(-1), num_segments=REPLICA_TOKENS + 1)[:REPLICA_TOKENS]
    return middle + low_back(mixture)

def adam_update(weight, moment, second, gradient, step_rate, decay_rate):
    moment_new = first_decay * moment + (1.0 - first_decay) * gradient
    second_new = second_decay * second + (1.0 - second_decay) * gradient * gradient
    step_size = step_rate / (1.0 - first_decay ** STEP)
    denominator = jnp.sqrt(second_new / (1.0 - second_decay ** STEP)) + adam_epsilon
    weight_new = weight - step_size * moment_new / denominator - step_rate * decay_rate * weight
    return (moment_new, second_new, weight_new)

def reference(inputs, cotangent, routes, gate_probs, seq_ids, norm_gains, gain_moment, gain_second, query_weight, query_moment, query_second, key_value_matrix, key_value_first_moment, key_value_second_moment, out_weight, out_moment, out_second, gate_up_weight, gate_up_moment, gate_up_second, down_weight, down_moment, down_second):
    params = (norm_gains, query_weight, key_value_matrix, out_weight, gate_up_weight, down_weight)
    moments = (gain_moment, query_moment, key_value_first_moment, out_moment, gate_up_moment, down_moment)
    seconds = (gain_second, query_second, key_value_second_moment, out_second, gate_up_second, down_second)
    scan_items = (inputs.astype(jnp.float32).reshape(N_DP, REPLICA_TOKENS, MODEL_WIDTH), cotangent.astype(jnp.float32).reshape(N_DP, REPLICA_TOKENS, MODEL_WIDTH), routes.reshape(N_DP, REPLICA_TOKENS, TOP), gate_probs.reshape(N_DP, REPLICA_TOKENS, TOP), seq_ids.reshape(N_DP, REPLICA_TOKENS))

    def replica(grad_total, part_items):
        part_in, part_cot, part_routes, part_probs, part_seq = part_items

        def run_forward(param_set, value_rows):
            return forward(param_set, value_rows, part_routes, part_probs, part_seq)
        result, pullback = jax.vjp(run_forward, params, part_in)
        gradients, grad_in = pullback(part_cot)
        return (jax.tree.map(jnp.add, grad_total, gradients), (result.astype(jnp.bfloat16), grad_in))
    gradients, (outputs, input_grads) = lax.scan(replica, jax.tree.map(jnp.zeros_like, params), scan_items)
    step_rates = (0.5, 1.5 * MODEL_WIDTH ** (-0.5), 1.5 * MODEL_WIDTH ** (-0.5), 1.5 * max(1, QUERY_HEADS * HEAD_SIZE // 256) ** (-0.5), 1.5 * MODEL_WIDTH ** (-0.5), 1.5 * (FF // 16) ** (-0.5))
    decay_rates = (0.0, weight_decay, weight_decay, weight_decay, weight_decay, weight_decay)
    updated = [adam_update(params[param_index], moments[param_index], seconds[param_index], gradients[param_index], step_rates[param_index], decay_rates[param_index]) for param_index in range(6)]
    return (outputs.reshape(TOKEN_TOTAL, MODEL_WIDTH), input_grads.reshape(TOKEN_TOTAL, MODEL_WIDTH), updated[0][0], updated[0][1], updated[0][2], updated[1][0], updated[1][1], updated[1][2], updated[2][0], updated[2][1], updated[2][2], updated[3][0], updated[3][1], updated[3][2], updated[4][0], updated[4][1], updated[4][2], updated[5][0], updated[5][1], updated[5][2])
```

```python
import jax
import jax.numpy as jnp
from jax import lax
from jax.sharding import PartitionSpec as P

MODEL_WIDTH = 1024
QUERY_HEADS = 16
KEY_VALUE_HEADS = 8
HEAD_SIZE = 64
FF = 512
EXPERTS = 32
TOP = 8
STEP = 10


norm_epsilon = 1e-06
first_decay = 0.9
second_decay = 0.95
adam_epsilon = 1e-08
weight_decay = 0.1
masked_score = -1e30
grid_axes = ("row", "col")
query_block = 384


def low(value):
    return value.astype(jnp.bfloat16)


def product(formula, left, right):
    return jnp.einsum(formula, left, right, preferred_element_type=jnp.float32)


def grid_split(rows):
    row_count, col_count = lax.axis_size("row"), lax.axis_size("col")
    tokens, width = rows.shape
    blocks = rows.reshape(row_count, tokens // row_count, col_count, width // col_count)
    return blocks.transpose(0, 2, 1, 3).reshape(
        row_count * col_count, tokens // row_count, width // col_count
    )


def grid_whole(block):
    row_count, col_count = lax.axis_size("row"), lax.axis_size("col")
    tokens, width = block.shape
    blocks = lax.all_gather(block, grid_axes, axis=0, tiled=False)
    blocks = blocks.reshape(row_count, col_count, tokens, width).transpose(0, 2, 1, 3)
    return blocks.reshape(row_count * tokens, col_count * width)


def grid_exchange(blocks):
    return lax.all_to_all(blocks, grid_axes, split_axis=0, concat_axis=0, tiled=True)


def col_exchange(blocks):
    return lax.all_to_all(blocks, "col", split_axis=0, concat_axis=0, tiled=True)


def grid_total(blocks):
    return lax.psum_scatter(blocks, grid_axes, scatter_dimension=0, tiled=True)


def own_rows(value_rows, index, count):
    return lax.dynamic_slice_in_dim(value_rows, index * count, count, axis=0)


def whole_experts(blocks):
    grid = lax.axis_size("row") * lax.axis_size("col")
    if blocks.shape[0] % grid == 0:
        split = blocks.reshape(-1, grid, *blocks.shape[1:]).swapaxes(0, 1)
        return grid_exchange(split).swapaxes(0, 1), True
    every = lax.all_gather(blocks, "dp", axis=0, tiled=True)
    split = every.reshape(-1, grid, *every.shape[1:]).swapaxes(0, 1)
    return grid_exchange(split).swapaxes(0, 1), False


def expert_blocks(grads, experts_here):
    grid = grads.shape[1]
    if experts_here % grid == 0:
        mine = lax.psum_scatter(grads, "dp", scatter_dimension=0, tiled=True)
        mine = grid_exchange(mine.swapaxes(0, 1)).swapaxes(0, 1)
        return mine.reshape(experts_here, *grads.shape[2:])
    every = grid_exchange(grads.swapaxes(0, 1)).swapaxes(0, 1)
    every = every.reshape(-1, *grads.shape[2:])
    return lax.psum_scatter(every, "dp", scatter_dimension=0, tiled=True)


def attend(query_rows, key_rows, value_rows, allowed_blocks, scale_factor):
    contexts, totals = [], []
    tokens = key_rows.shape[0]
    for start in range(0, tokens, query_block):
        stop = start + query_block
        scores = product("gqd,td->gqt", query_rows[:, start:stop], key_rows[:stop]) * scale_factor
        scores = jnp.where(allowed_blocks[start // query_block], scores, masked_score)
        row_max = jnp.max(scores, axis=-1, keepdims=True)
        log_total = row_max + jnp.log(jnp.sum(jnp.exp(scores - row_max), axis=-1, keepdims=True))
        prob_low = low(jnp.exp(scores - log_total))
        contexts.append(low(product("gqt,td->gqd", prob_low, value_rows[:stop])))
        totals.append(log_total)
    return jnp.concatenate(contexts, axis=1), totals


def attend_back(query_rows, key_rows, value_rows, grad_rows, totals, allowed_blocks, scale_factor):
    tokens = key_rows.shape[0]
    grad_queries = []
    grad_keys = jnp.zeros(key_rows.shape, jnp.float32)
    grad_values = jnp.zeros(key_rows.shape, jnp.float32)
    for start in range(0, tokens, query_block):
        stop = start + query_block
        block_query = query_rows[:, start:stop]
        block_grad = grad_rows[:, start:stop]
        scores = product("gqd,td->gqt", block_query, key_rows[:stop]) * scale_factor
        scores = jnp.where(allowed_blocks[start // query_block], scores, masked_score)
        full = jnp.exp(scores - totals[start // query_block])
        grad_prob = product("gqd,td->gqt", block_grad, value_rows[:stop])
        inner = jnp.sum(full * grad_prob, axis=-1, keepdims=True)
        grad_scores = low(full * (grad_prob - inner))
        grad_queries.append(product("gqt,td->gqd", grad_scores, key_rows[:stop]) * scale_factor)
        rest = ((0, tokens - stop), (0, 0))
        grad_keys = grad_keys + jnp.pad(product("gqt,gqd->td", grad_scores, block_query), rest)
        grad_values = grad_values + jnp.pad(product("gqt,gqd->td", low(full), block_grad), rest)
    return jnp.concatenate(grad_queries, axis=1), grad_keys * scale_factor, grad_values


def adam_update(weight, moment, second, gradient, step_rate, decay_rate):
    moment_new = first_decay * moment + (1.0 - first_decay) * gradient
    second_new = second_decay * second + (1.0 - second_decay) * gradient * gradient
    step_size = step_rate / (1.0 - first_decay**STEP)
    denominator = jnp.sqrt(second_new / (1.0 - second_decay**STEP)) + adam_epsilon
    weight_new = weight - step_size * moment_new / denominator - step_rate * decay_rate * weight
    return (moment_new, second_new, weight_new)


def per_device(
    inputs,
    cotangent,
    routes,
    gate_probs,
    seq_ids,
    norm_gains,
    gain_moment,
    gain_second,
    query_weight,
    query_moment,
    query_second,
    key_value_matrix,
    key_value_first_moment,
    key_value_second_moment,
    out_weight,
    out_moment,
    out_second,
    gate_up_weight,
    gate_up_moment,
    gate_up_second,
    down_weight,
    down_moment,
    down_second,
):
    rep_tokens = routes.shape[0]
    row_count, col_count = lax.axis_size("row"), lax.axis_size("col")
    grid = row_count * col_count
    row_index, col_index = lax.axis_index("row"), lax.axis_index("col")
    place = row_index * col_count + col_index
    width_part = inputs.shape[1]
    key_width = key_value_matrix.shape[2]
    group_width = QUERY_HEADS // KEY_VALUE_HEADS
    head_span = group_width * HEAD_SIZE
    scale_factor = HEAD_SIZE ** (-0.5)
    capacity = rep_tokens * TOP // EXPERTS * 5 // 4
    own_count = EXPERTS // grid
    part_tokens = rep_tokens // grid
    half_tokens = rep_tokens // row_count
    ff_part = down_weight.shape[1]
    experts_here = gate_up_weight.shape[0]
    heads_here = key_width // HEAD_SIZE
    weight_in_here = low(
        jnp.concatenate(
            [
                query_weight.reshape(width_part, heads_here, head_span),
                key_value_matrix[0].reshape(width_part, heads_here, HEAD_SIZE),
                key_value_matrix[1].reshape(width_part, heads_here, HEAD_SIZE),
            ],
            axis=2,
        )
    ).transpose(1, 0, 2)
    head_width = weight_in_here.shape[2]
    inputs_all = grid_whole(inputs)
    weight_in_all = lax.all_gather(weight_in_here, grid_axes, axis=0, tiled=False)
    weight_in_all = (
        weight_in_all.reshape(row_count, col_count, heads_here, width_part, head_width)
        .transpose(0, 2, 1, 3, 4)
        .reshape(grid, MODEL_WIDTH, head_width)
    )
    weight_in = lax.dynamic_index_in_dim(weight_in_all, place, axis=0, keepdims=False)
    out_all = grid_whole(low(out_weight))
    expert_weights = low(
        jnp.concatenate(
            [gate_up_weight.reshape(experts_here, width_part, 2 * ff_part), down_weight], axis=2
        )
    )
    expert_weights, spread = whole_experts(expert_weights)
    gate_up_mine = (
        expert_weights[..., : 2 * ff_part]
        .reshape(-1, row_count, col_count * width_part, 2, ff_part)
        .transpose(0, 2, 3, 1, 4)
        .reshape(-1, MODEL_WIDTH, 2 * FF)
    )
    down_mine = (
        expert_weights[..., 2 * ff_part :]
        .reshape(-1, row_count, col_count, ff_part, width_part)
        .transpose(0, 1, 3, 2, 4)
        .reshape(-1, FF, MODEL_WIDTH)
    )
    if spread:
        gate_up_mine = lax.all_gather(gate_up_mine, "dp", axis=0, tiled=True)
        down_mine = lax.all_gather(down_mine, "dp", axis=0, tiled=True)
    cotangent_all = grid_whole(cotangent)
    gains_all = lax.all_gather(norm_gains, "col", axis=1, tiled=True)

    own_ids = jnp.arange(own_count, dtype=jnp.int32) * grid + place
    named = routes[:, :, None] == own_ids[None, None, :]
    token_weights = jnp.sum(jnp.where(named, gate_probs[:, :, None], 0.0), axis=1)
    chosen = jnp.any(named, axis=1)
    positions = jnp.arange(rep_tokens, dtype=jnp.int32)
    earlier = low(positions[:, None] > positions[None, :])
    slot_of = product("ts,si->it", earlier, low(chosen)).astype(jnp.int32)
    slot_of = jnp.where(chosen.T, slot_of, -1)
    slots = jnp.arange(capacity, dtype=jnp.int32)
    filled = slot_of[:, None, :] == slots[None, :, None]
    slot_weights = jnp.sum(jnp.where(filled, token_weights.T[:, None, :], 0.0), axis=2)[..., None]
    pick = low(filled)

    residual = inputs_all.astype(jnp.float32)
    first_scale = lax.rsqrt(jnp.mean(residual * residual, axis=1, keepdims=True) + norm_epsilon)
    normed = low(residual * first_scale * gains_all[0])
    projected = low(product("td,df->tf", normed, weight_in))
    query_rows = projected[:, :head_span].reshape(rep_tokens, group_width, HEAD_SIZE)
    query_rows = query_rows.transpose(1, 0, 2)
    key_rows = projected[:, head_span : head_span + HEAD_SIZE]
    value_rows = projected[:, head_span + HEAD_SIZE :]
    allowed_blocks = [
        (seq_ids[start : start + query_block, None] == seq_ids[None, : start + query_block])
        & (
            positions[None, : start + query_block]
            <= positions[start : start + query_block, None]
        )
        for start in range(0, rep_tokens, query_block)
    ]
    context, totals = attend(query_rows, key_rows, value_rows, allowed_blocks, scale_factor)
    context = context.transpose(1, 0, 2).reshape(rep_tokens, head_span)
    context_all = lax.all_gather(context, grid_axes, axis=1, tiled=True)
    middle = residual + product("th,hd->td", context_all, out_all)
    second_scale = lax.rsqrt(jnp.mean(middle * middle, axis=1, keepdims=True) + norm_epsilon)
    normed_two = low(middle * second_scale * gains_all[1])

    slot_inputs = low(product("ist,td->isd", pick, normed_two))
    gate_up = product("isd,idf->isf", slot_inputs, gate_up_mine)
    gate_part, up_part = gate_up[..., :FF], gate_up[..., FF:]
    hidden = low(jax.nn.silu(gate_part) * up_part)
    expert_out = low(product("isf,ifd->isd", hidden, down_mine) * slot_weights)
    mixture = low(product("ist,isd->td", pick, expert_out))
    mixture = grid_total(grid_split(mixture).reshape(-1, width_part))
    middle_here = lax.dynamic_slice(
        middle, (row_index * half_tokens, col_index * width_part), (half_tokens, width_part)
    )
    block_output = low(middle_here + mixture.astype(jnp.float32))

    grad_slots = low(product("ist,td->isd", pick, cotangent_all) * slot_weights)
    grad_hidden = product("isd,ifd->isf", grad_slots, down_mine)
    sigmoid_gate = jax.nn.sigmoid(gate_part)
    grad_gate = grad_hidden * up_part * sigmoid_gate * (1.0 + gate_part * (1.0 - sigmoid_gate))
    grad_up = grad_hidden * gate_part * sigmoid_gate
    grad_pair = low(jnp.concatenate([grad_gate, grad_up], axis=2))
    back_slots = low(product("isf,idf->isd", grad_pair, gate_up_mine))
    grad_normed_two = low(product("ist,isd->td", pick, back_slots))
    grad_normed_two = grid_total(grad_normed_two).astype(jnp.float32)
    down_grads = low(product("isf,isd->ifd", hidden, grad_slots))
    gate_up_grads = low(product("isd,isf->idf", slot_inputs, grad_pair))
    gate_up_grads = gate_up_grads.reshape(
        own_count, col_count, width_part, 2, row_count, ff_part
    ).transpose(0, 4, 1, 2, 3, 5)
    gate_up_grads = gate_up_grads.reshape(own_count, grid, width_part, 2 * ff_part)
    down_grads = down_grads.reshape(
        own_count, row_count, ff_part, col_count, width_part
    ).transpose(0, 1, 3, 2, 4)
    down_grads = down_grads.reshape(own_count, grid, ff_part, width_part)
    grad_gate_up = expert_blocks(gate_up_grads, experts_here).astype(jnp.float32)
    grad_gate_up = grad_gate_up.reshape(gate_up_weight.shape)
    grad_down = expert_blocks(down_grads, experts_here).astype(jnp.float32)

    middle_part = own_rows(middle, place, part_tokens)
    scale_part = own_rows(second_scale, place, part_tokens)
    inner = jnp.sum(grad_normed_two * gains_all[1] * middle_part, axis=1, keepdims=True)
    grad_middle = (
        own_rows(cotangent_all, place, part_tokens).astype(jnp.float32)
        + scale_part * gains_all[1] * grad_normed_two
        - middle_part * scale_part**3 * inner / MODEL_WIDTH
    )
    grad_gain_two = jnp.sum(grad_normed_two * middle_part * scale_part, axis=0)
    grad_middle_all = lax.all_gather(low(grad_middle), grid_axes, axis=0, tiled=True)

    out_mine = own_rows(out_all, place, head_span)
    grad_context = low(product("td,hd->th", grad_middle_all, out_mine))
    out_grads = product("th,td->hd", context, grad_middle_all)
    grad_context = grad_context.reshape(rep_tokens, group_width, HEAD_SIZE).transpose(1, 0, 2)
    grad_queries, grad_keys, grad_values = attend_back(
        query_rows, key_rows, value_rows, grad_context, totals, allowed_blocks, scale_factor
    )
    grad_queries = grad_queries.transpose(1, 0, 2).reshape(rep_tokens, head_span)
    grad_in = low(jnp.concatenate([grad_queries, grad_keys, grad_values], axis=1))
    grad_in_part = grid_exchange(grad_in.reshape(grid, part_tokens, head_width))
    weight_in_grads = product("td,tf->df", normed, grad_in)
    grad_normed = product("htf,hdf->td", grad_in_part, weight_in_all)

    residual_part = own_rows(residual, place, part_tokens)
    scale_part = own_rows(first_scale, place, part_tokens)
    inner = jnp.sum(grad_normed * gains_all[0] * residual_part, axis=1, keepdims=True)
    input_grad = (
        grad_middle
        + scale_part * gains_all[0] * grad_normed
        - residual_part * scale_part**3 * inner / MODEL_WIDTH
    )
    grad_gain_one = jnp.sum(grad_normed * residual_part * scale_part, axis=0)
    input_grad = input_grad.reshape(part_tokens, col_count, width_part).transpose(1, 0, 2)
    input_grad = col_exchange(input_grad).reshape(half_tokens, width_part)
    gain_grad = lax.psum(jnp.stack([grad_gain_one, grad_gain_two]), ("dp", "row", "col"))
    gain_grad = lax.dynamic_slice_in_dim(gain_grad, col_index * width_part, width_part, axis=1)

    head_blocks = jnp.concatenate(
        [
            low(weight_in_grads).reshape(col_count, width_part, head_width),
            low(out_grads)
            .reshape(head_span, col_count, width_part)
            .transpose(1, 2, 0),
        ],
        axis=2,
    )
    head_blocks = col_exchange(head_blocks)
    head_blocks = lax.psum(head_blocks, "dp").astype(jnp.float32)
    query_grad = head_blocks[..., :head_span].transpose(1, 0, 2).reshape(query_weight.shape)
    key_value_grad = jnp.stack(
        [
            head_blocks[..., head_span : head_span + HEAD_SIZE],
            head_blocks[..., head_span + HEAD_SIZE : head_width],
        ]
    ).transpose(0, 2, 1, 3)
    key_value_grad = key_value_grad.reshape(key_value_matrix.shape)
    out_grad = head_blocks[..., head_width:].transpose(0, 2, 1).reshape(out_weight.shape)
    matrix_rate = 1.5 * MODEL_WIDTH ** (-0.5)
    gains_moment_new, gains_second_new, gains_new = adam_update(
        norm_gains, gain_moment, gain_second, gain_grad, 0.5, 0.0
    )
    query_moment_new, query_second_new, query_new = adam_update(
        query_weight, query_moment, query_second, query_grad, matrix_rate, weight_decay
    )
    pair_moment_new, pair_second_new, pair_new = adam_update(
        key_value_matrix,
        key_value_first_moment,
        key_value_second_moment,
        key_value_grad,
        matrix_rate,
        weight_decay,
    )
    out_moment_new, out_second_new, out_new = adam_update(
        out_weight,
        out_moment,
        out_second,
        out_grad,
        1.5 * max(1, QUERY_HEADS * HEAD_SIZE // 256) ** (-0.5),
        weight_decay,
    )
    gate_moment_new, gate_second_new, gate_new = adam_update(
        gate_up_weight, gate_up_moment, gate_up_second, grad_gate_up, matrix_rate, weight_decay
    )
    down_moment_new, down_second_new, down_new = adam_update(
        down_weight, down_moment, down_second, grad_down, 1.5 * (FF // 16) ** (-0.5), weight_decay
    )
    return (
        block_output,
        input_grad,
        gains_moment_new,
        gains_second_new,
        gains_new,
        query_moment_new,
        query_second_new,
        query_new,
        pair_moment_new,
        pair_second_new,
        pair_new,
        out_moment_new,
        out_second_new,
        out_new,
        gate_moment_new,
        gate_second_new,
        gate_new,
        down_moment_new,
        down_second_new,
        down_new,
    )


def solution(mesh):
    return jax.shard_map(
        per_device,
        mesh=mesh,
        in_specs=(
            P(("dp", "row"), "col"),
            P(("dp", "row"), "col"),
            P("dp", None),
            P("dp", None),
            P("dp"),
            P(None, "col"),
            P(None, "col"),
            P(None, "col"),
            P("col", "row"),
            P("col", "row"),
            P("col", "row"),
            P(None, "col", "row"),
            P(None, "col", "row"),
            P(None, "col", "row"),
            P("row", "col"),
            P("row", "col"),
            P("row", "col"),
            P("dp", "col", None, "row"),
            P("dp", "col", None, "row"),
            P("dp", "col", None, "row"),
            P("dp", "row", "col"),
            P("dp", "row", "col"),
            P("dp", "row", "col"),
        ),
        out_specs=(
            P(("dp", "row"), "col"),
            P(("dp", "row"), "col"),
            P(None, "col"),
            P(None, "col"),
            P(None, "col"),
            P("col", "row"),
            P("col", "row"),
            P("col", "row"),
            P(None, "col", "row"),
            P(None, "col", "row"),
            P(None, "col", "row"),
            P("row", "col"),
            P("row", "col"),
            P("row", "col"),
            P("dp", "col", None, "row"),
            P("dp", "col", None, "row"),
            P("dp", "col", None, "row"),
            P("dp", "row", "col"),
            P("dp", "row", "col"),
            P("dp", "row", "col"),
        ),
        check_vma=False,
    )
```

```python
import jax
import jax.numpy as jnp
from jax import lax
from jax.sharding import PartitionSpec as P

MODEL_WIDTH = 1024
QUERY_HEADS = 16
KEY_VALUE_HEADS = 8
HEAD_SIZE = 64
FF = 512
EXPERTS = 32
TOP = 8
STEP = 10


norm_epsilon = 1e-06
first_decay = 0.9
second_decay = 0.95
adam_epsilon = 1e-08
weight_decay = 0.1
masked_score = -1e30
grid_axes = ("row", "col")
query_block = 384


def low(value):
    return value.astype(jnp.bfloat16)


def product(formula, left, right):
    return jnp.einsum(formula, left, right, preferred_element_type=jnp.float32)


def grid_split(rows):
    row_count, col_count = lax.axis_size("row"), lax.axis_size("col")
    tokens, width = rows.shape
    blocks = rows.reshape(row_count, tokens // row_count, col_count, width // col_count)
    return blocks.transpose(0, 2, 1, 3).reshape(
        row_count * col_count, tokens // row_count, width // col_count
    )


def copies(block, axes):
    count = 1
    for axis in axes:
        count *= lax.axis_size(axis)
    equal = jnp.broadcast_to(block[None], (count, *block.shape))
    return lax.all_to_all(equal, axes, split_axis=0, concat_axis=0, tiled=True)


def grid_whole(block, gather):
    row_count, col_count = lax.axis_size("row"), lax.axis_size("col")
    tokens, width = block.shape
    blocks = gather(block)
    blocks = blocks.reshape(row_count, col_count, tokens, width).transpose(0, 2, 1, 3)
    return blocks.reshape(row_count * tokens, col_count * width)


def grid_exchange(blocks):
    return lax.all_to_all(blocks, grid_axes, split_axis=0, concat_axis=0, tiled=True)


def col_exchange(blocks):
    return lax.all_to_all(blocks, "col", split_axis=0, concat_axis=0, tiled=True)


def gathered(block):
    return lax.all_gather(block, grid_axes, axis=0, tiled=False)


def copied(block):
    return copies(block, grid_axes)


def grid_total(blocks):
    return lax.psum_scatter(blocks, grid_axes, scatter_dimension=0, tiled=True)


def own_rows(value_rows, index, count):
    return lax.dynamic_slice_in_dim(value_rows, index * count, count, axis=0)


def whole_experts(blocks):
    grid = lax.axis_size("row") * lax.axis_size("col")
    if blocks.shape[0] % grid == 0:
        split = blocks.reshape(-1, grid, *blocks.shape[1:]).swapaxes(0, 1)
        return grid_exchange(split).swapaxes(0, 1), True
    every = lax.all_gather(blocks, "dp", axis=0, tiled=True)
    split = every.reshape(-1, grid, *every.shape[1:]).swapaxes(0, 1)
    return grid_exchange(split).swapaxes(0, 1), False


def expert_blocks(grads, experts_here):
    grid = grads.shape[1]
    if experts_here % grid == 0:
        dp_count = lax.axis_size("dp")
        parts = lax.all_to_all(grads, "dp", split_axis=0, concat_axis=0, tiled=True)
        parts = parts.reshape(dp_count, -1, *grads.shape[1:])
        mine = low(jnp.sum(parts.astype(jnp.float32), axis=0))
        mine = grid_exchange(mine.swapaxes(0, 1)).swapaxes(0, 1)
        return mine.reshape(experts_here, *grads.shape[2:])
    every = grid_exchange(grads.swapaxes(0, 1)).swapaxes(0, 1)
    every = every.reshape(-1, *grads.shape[2:])
    return lax.psum_scatter(every, "dp", scatter_dimension=0, tiled=True)


def attend(query_rows, key_rows, value_rows, allowed_blocks, scale_factor):
    contexts, totals = [], []
    tokens = key_rows.shape[0]
    for start in range(0, tokens, query_block):
        stop = start + query_block
        scores = product("gqd,td->gqt", query_rows[:, start:stop], key_rows[:stop]) * scale_factor
        scores = jnp.where(allowed_blocks[start // query_block], scores, masked_score)
        row_max = jnp.max(scores, axis=-1, keepdims=True)
        log_total = row_max + jnp.log(jnp.sum(jnp.exp(scores - row_max), axis=-1, keepdims=True))
        prob_low = low(jnp.exp(scores - log_total))
        contexts.append(low(product("gqt,td->gqd", prob_low, value_rows[:stop])))
        totals.append(log_total)
    return jnp.concatenate(contexts, axis=1), totals


def attend_back(query_rows, key_rows, value_rows, grad_rows, totals, allowed_blocks, scale_factor):
    tokens = key_rows.shape[0]
    grad_queries = []
    grad_keys = jnp.zeros(key_rows.shape, jnp.float32)
    grad_values = jnp.zeros(key_rows.shape, jnp.float32)
    for start in range(0, tokens, query_block):
        stop = start + query_block
        block_query = query_rows[:, start:stop]
        block_grad = grad_rows[:, start:stop]
        scores = product("gqd,td->gqt", block_query, key_rows[:stop]) * scale_factor
        scores = jnp.where(allowed_blocks[start // query_block], scores, masked_score)
        full = jnp.exp(scores - totals[start // query_block])
        grad_prob = product("gqd,td->gqt", block_grad, value_rows[:stop])
        inner = jnp.sum(full * grad_prob, axis=-1, keepdims=True)
        grad_scores = low(full * (grad_prob - inner))
        grad_queries.append(product("gqt,td->gqd", grad_scores, key_rows[:stop]) * scale_factor)
        rest = ((0, tokens - stop), (0, 0))
        grad_keys = grad_keys + jnp.pad(product("gqt,gqd->td", grad_scores, block_query), rest)
        grad_values = grad_values + jnp.pad(product("gqt,gqd->td", low(full), block_grad), rest)
    return jnp.concatenate(grad_queries, axis=1), grad_keys * scale_factor, grad_values


def adam_update(weight, moment, second, gradient, step_rate, decay_rate):
    moment_new = first_decay * moment + (1.0 - first_decay) * gradient
    second_new = second_decay * second + (1.0 - second_decay) * gradient * gradient
    step_size = step_rate / (1.0 - first_decay**STEP)
    denominator = jnp.sqrt(second_new / (1.0 - second_decay**STEP)) + adam_epsilon
    weight_new = weight - step_size * moment_new / denominator - step_rate * decay_rate * weight
    return (moment_new, second_new, weight_new)


def per_device(
    inputs,
    cotangent,
    routes,
    gate_probs,
    seq_ids,
    norm_gains,
    gain_moment,
    gain_second,
    query_weight,
    query_moment,
    query_second,
    key_value_matrix,
    key_value_first_moment,
    key_value_second_moment,
    out_weight,
    out_moment,
    out_second,
    gate_up_weight,
    gate_up_moment,
    gate_up_second,
    down_weight,
    down_moment,
    down_second,
):
    rep_tokens = routes.shape[0]
    row_count, col_count = lax.axis_size("row"), lax.axis_size("col")
    grid = row_count * col_count
    row_index, col_index = lax.axis_index("row"), lax.axis_index("col")
    place = row_index * col_count + col_index
    width_part = inputs.shape[1]
    key_width = key_value_matrix.shape[2]
    group_width = QUERY_HEADS // KEY_VALUE_HEADS
    head_span = group_width * HEAD_SIZE
    scale_factor = HEAD_SIZE ** (-0.5)
    capacity = rep_tokens * TOP // EXPERTS * 5 // 4
    own_count = EXPERTS // grid
    part_tokens = rep_tokens // grid
    half_tokens = rep_tokens // row_count
    ff_part = down_weight.shape[1]
    experts_here = gate_up_weight.shape[0]
    heads_here = key_width // HEAD_SIZE
    weight_in_here = low(
        jnp.concatenate(
            [
                query_weight.reshape(width_part, heads_here, head_span),
                key_value_matrix[0].reshape(width_part, heads_here, HEAD_SIZE),
                key_value_matrix[1].reshape(width_part, heads_here, HEAD_SIZE),
            ],
            axis=2,
        )
    ).transpose(1, 0, 2)
    head_width = weight_in_here.shape[2]
    inputs_all = grid_whole(inputs, gathered)
    weight_in = col_exchange(weight_in_here).reshape(MODEL_WIDTH, head_width)
    out_all = grid_whole(low(out_weight), copied)
    expert_weights = low(
        jnp.concatenate(
            [gate_up_weight.reshape(experts_here, width_part, 2 * ff_part), down_weight], axis=2
        )
    )
    expert_weights, spread = whole_experts(expert_weights)
    gate_up_mine = (
        expert_weights[..., : 2 * ff_part]
        .reshape(-1, row_count, col_count * width_part, 2 * ff_part)
        .transpose(0, 2, 1, 3)
        .reshape(-1, MODEL_WIDTH, 2 * FF)
    )
    down_mine = (
        expert_weights[..., 2 * ff_part :]
        .reshape(-1, row_count, col_count, ff_part, width_part)
        .transpose(0, 1, 3, 2, 4)
        .reshape(-1, FF, MODEL_WIDTH)
    )
    inputs_all, gate_up_mine = lax.optimization_barrier((inputs_all, gate_up_mine))
    if spread:
        gate_up_mine = lax.all_gather(gate_up_mine, "dp", axis=0, tiled=True)
        down_mine = lax.all_gather(down_mine, "dp", axis=0, tiled=True)
    cotangent_all = grid_whole(cotangent, copied)
    gains_all = copies(norm_gains, ("col",)).transpose(1, 0, 2).reshape(2, MODEL_WIDTH)

    own_ids = jnp.arange(own_count, dtype=jnp.int32) * grid + place
    named = routes[:, :, None] == own_ids[None, None, :]
    token_weights = jnp.sum(jnp.where(named, gate_probs[:, :, None], 0.0), axis=1)
    chosen = jnp.any(named, axis=1)
    positions = jnp.arange(rep_tokens, dtype=jnp.int32)
    earlier = low(positions[:, None] > positions[None, :])
    slot_of = product("ts,si->it", earlier, low(chosen)).astype(jnp.int32)
    slot_of = jnp.where(chosen.T, slot_of, -1)
    slots = jnp.arange(capacity, dtype=jnp.int32)
    filled = slot_of[:, None, :] == slots[None, :, None]
    slot_weights = jnp.sum(jnp.where(filled, token_weights.T[:, None, :], 0.0), axis=2)[..., None]
    pick = low(filled)

    residual = inputs_all.astype(jnp.float32)
    first_scale = lax.rsqrt(jnp.mean(residual * residual, axis=1, keepdims=True) + norm_epsilon)
    normed = low(residual * first_scale * gains_all[0])
    projected = low(product("td,df->tf", normed, weight_in))
    query_rows = projected[:, :head_span].reshape(rep_tokens, group_width, HEAD_SIZE)
    query_rows = query_rows.transpose(1, 0, 2)
    key_rows = projected[:, head_span : head_span + HEAD_SIZE]
    value_rows = projected[:, head_span + HEAD_SIZE :]
    allowed_blocks = [
        (seq_ids[start : start + query_block, None] == seq_ids[None, : start + query_block])
        & (
            positions[None, : start + query_block]
            <= positions[start : start + query_block, None]
        )
        for start in range(0, rep_tokens, query_block)
    ]
    context, totals = attend(query_rows, key_rows, value_rows, allowed_blocks, scale_factor)
    context = context.transpose(1, 0, 2).reshape(rep_tokens, head_span)
    context_all = lax.all_gather(context, grid_axes, axis=1, tiled=True)
    middle = residual + product("th,hd->td", context_all, out_all)
    second_scale = lax.rsqrt(jnp.mean(middle * middle, axis=1, keepdims=True) + norm_epsilon)
    normed_two = low(middle * second_scale * gains_all[1])

    slot_inputs = low(product("ist,td->isd", pick, normed_two))
    gate_up = product("isd,idf->isf", slot_inputs, gate_up_mine)
    gate_part = jnp.concatenate(
        [gate_up[..., 2 * r * ff_part : (2 * r + 1) * ff_part] for r in range(row_count)], axis=2
    )
    up_part = jnp.concatenate(
        [gate_up[..., (2 * r + 1) * ff_part : (2 * r + 2) * ff_part] for r in range(row_count)],
        axis=2,
    )
    hidden = low(jax.nn.silu(gate_part) * up_part)
    expert_out = low(product("isf,ifd->isd", hidden, down_mine) * slot_weights)
    mixture = low(product("ist,isd->td", pick, expert_out))
    mixture = grid_exchange(grid_split(mixture))
    mixture = jnp.sum(mixture.astype(jnp.float32), axis=0)
    middle_here = lax.dynamic_slice(
        middle, (row_index * half_tokens, col_index * width_part), (half_tokens, width_part)
    )
    block_output = low(middle_here + mixture)

    grad_slots = low(product("ist,td->isd", pick, cotangent_all) * slot_weights)
    grad_hidden = product("isd,ifd->isf", grad_slots, down_mine)
    sigmoid_gate = jax.nn.sigmoid(gate_part)
    grad_gate = grad_hidden * up_part * sigmoid_gate * (1.0 + gate_part * (1.0 - sigmoid_gate))
    grad_up = grad_hidden * gate_part * sigmoid_gate
    grad_pair = low(
        jnp.concatenate(
            [
                side[..., r * ff_part : (r + 1) * ff_part]
                for r in range(row_count)
                for side in (grad_gate, grad_up)
            ],
            axis=2,
        )
    )
    back_slots = low(product("isf,idf->isd", grad_pair, gate_up_mine))
    grad_normed_two = low(product("ist,isd->td", pick, back_slots))
    grad_normed_two = grid_total(grad_normed_two).astype(jnp.float32)
    down_grads = low(product("isf,isd->ifd", hidden, grad_slots))
    gate_up_grads = low(product("isd,isf->idf", slot_inputs, grad_pair))
    gate_up_grads = gate_up_grads.reshape(
        own_count, col_count, width_part, row_count, 2 * ff_part
    ).transpose(0, 3, 1, 2, 4)
    gate_up_grads = gate_up_grads.reshape(own_count, grid, width_part, 2 * ff_part)
    down_grads = down_grads.reshape(
        own_count, row_count, ff_part, col_count, width_part
    ).transpose(0, 1, 3, 2, 4)
    down_grads = down_grads.reshape(own_count, grid, ff_part, width_part)
    grad_gate_up = expert_blocks(gate_up_grads, experts_here).astype(jnp.float32)
    grad_gate_up = grad_gate_up.reshape(gate_up_weight.shape)
    grad_down = expert_blocks(down_grads, experts_here).astype(jnp.float32)

    middle_part = own_rows(middle, place, part_tokens)
    scale_part = own_rows(second_scale, place, part_tokens)
    inner = jnp.sum(grad_normed_two * gains_all[1] * middle_part, axis=1, keepdims=True)
    grad_middle = (
        own_rows(cotangent_all, place, part_tokens).astype(jnp.float32)
        + scale_part * gains_all[1] * grad_normed_two
        - middle_part * scale_part**3 * inner / MODEL_WIDTH
    )
    grad_gain_two = jnp.sum(grad_normed_two * middle_part * scale_part, axis=0)
    grad_middle_all = lax.all_gather(low(grad_middle), grid_axes, axis=0, tiled=True)

    weight_in_here, grad_middle = lax.optimization_barrier((weight_in_here, grad_middle))
    weight_in_all = lax.all_gather(weight_in_here, grid_axes, axis=0, tiled=False)
    weight_in_all = (
        weight_in_all.reshape(row_count, col_count, heads_here, width_part, head_width)
        .transpose(0, 2, 1, 3, 4)
        .reshape(grid, MODEL_WIDTH, head_width)
    )
    out_mine = own_rows(out_all, place, head_span)
    grad_context = low(product("td,hd->th", grad_middle_all, out_mine))
    out_grads = product("th,td->hd", context, grad_middle_all)
    grad_context = grad_context.reshape(rep_tokens, group_width, HEAD_SIZE).transpose(1, 0, 2)
    grad_queries, grad_keys, grad_values = attend_back(
        query_rows, key_rows, value_rows, grad_context, totals, allowed_blocks, scale_factor
    )
    grad_queries = grad_queries.transpose(1, 0, 2).reshape(rep_tokens, head_span)
    grad_in = low(jnp.concatenate([grad_queries, grad_keys, grad_values], axis=1))
    grad_in_part = grid_exchange(grad_in.reshape(grid, part_tokens, head_width))
    weight_in_grads = product("td,tf->df", normed, grad_in)
    grad_normed = product("htf,hdf->td", grad_in_part, weight_in_all)

    residual_part = own_rows(residual, place, part_tokens)
    scale_part = own_rows(first_scale, place, part_tokens)
    inner = jnp.sum(grad_normed * gains_all[0] * residual_part, axis=1, keepdims=True)
    input_grad = (
        grad_middle
        + scale_part * gains_all[0] * grad_normed
        - residual_part * scale_part**3 * inner / MODEL_WIDTH
    )
    grad_gain_one = jnp.sum(grad_normed * residual_part * scale_part, axis=0)
    input_grad = input_grad.reshape(part_tokens, col_count, width_part).transpose(1, 0, 2)
    input_grad = col_exchange(input_grad).reshape(half_tokens, width_part)
    gain_grad = jnp.stack([grad_gain_one, grad_gain_two]).reshape(2, col_count, width_part)
    gain_grad = jnp.broadcast_to(
        gain_grad.transpose(1, 0, 2), (lax.axis_size("dp") * row_count, col_count, 2, width_part)
    )
    gain_grad = lax.all_to_all(
        gain_grad.reshape(-1, 2, width_part),
        ("dp", "row", "col"),
        split_axis=0,
        concat_axis=0,
        tiled=True,
    )
    gain_grad = jnp.sum(gain_grad, axis=0)

    head_blocks = jnp.concatenate(
        [
            low(weight_in_grads).reshape(col_count, width_part, head_width),
            low(out_grads)
            .reshape(head_span, col_count, width_part)
            .transpose(1, 2, 0),
        ],
        axis=2,
    )
    head_blocks = col_exchange(head_blocks)
    if lax.axis_size("dp") <= 4:
        head_blocks = jnp.sum(copies(head_blocks, ("dp",)).astype(jnp.float32), axis=0)
    else:
        head_blocks = lax.psum(head_blocks, "dp").astype(jnp.float32)
    query_grad = head_blocks[..., :head_span].transpose(1, 0, 2).reshape(query_weight.shape)
    key_value_grad = jnp.stack(
        [
            head_blocks[..., head_span : head_span + HEAD_SIZE],
            head_blocks[..., head_span + HEAD_SIZE : head_width],
        ]
    ).transpose(0, 2, 1, 3)
    key_value_grad = key_value_grad.reshape(key_value_matrix.shape)
    out_grad = head_blocks[..., head_width:].transpose(0, 2, 1).reshape(out_weight.shape)
    matrix_rate = 1.5 * MODEL_WIDTH ** (-0.5)
    gains_moment_new, gains_second_new, gains_new = adam_update(
        norm_gains, gain_moment, gain_second, gain_grad, 0.5, 0.0
    )
    query_moment_new, query_second_new, query_new = adam_update(
        query_weight, query_moment, query_second, query_grad, matrix_rate, weight_decay
    )
    pair_moment_new, pair_second_new, pair_new = adam_update(
        key_value_matrix,
        key_value_first_moment,
        key_value_second_moment,
        key_value_grad,
        matrix_rate,
        weight_decay,
    )
    out_moment_new, out_second_new, out_new = adam_update(
        out_weight,
        out_moment,
        out_second,
        out_grad,
        1.5 * max(1, QUERY_HEADS * HEAD_SIZE // 256) ** (-0.5),
        weight_decay,
    )
    gate_moment_new, gate_second_new, gate_new = adam_update(
        gate_up_weight, gate_up_moment, gate_up_second, grad_gate_up, matrix_rate, weight_decay
    )
    down_moment_new, down_second_new, down_new = adam_update(
        down_weight, down_moment, down_second, grad_down, 1.5 * (FF // 16) ** (-0.5), weight_decay
    )
    return (
        block_output,
        input_grad,
        gains_moment_new,
        gains_second_new,
        gains_new,
        query_moment_new,
        query_second_new,
        query_new,
        pair_moment_new,
        pair_second_new,
        pair_new,
        out_moment_new,
        out_second_new,
        out_new,
        gate_moment_new,
        gate_second_new,
        gate_new,
        down_moment_new,
        down_second_new,
        down_new,
    )


def solution(mesh):
    return jax.shard_map(
        per_device,
        mesh=mesh,
        in_specs=(
            P(("dp", "row"), "col"),
            P(("dp", "row"), "col"),
            P("dp", None),
            P("dp", None),
            P("dp"),
            P(None, "col"),
            P(None, "col"),
            P(None, "col"),
            P("col", "row"),
            P("col", "row"),
            P("col", "row"),
            P(None, "col", "row"),
            P(None, "col", "row"),
            P(None, "col", "row"),
            P("row", "col"),
            P("row", "col"),
            P("row", "col"),
            P("dp", "col", None, "row"),
            P("dp", "col", None, "row"),
            P("dp", "col", None, "row"),
            P("dp", "row", "col"),
            P("dp", "row", "col"),
            P("dp", "row", "col"),
        ),
        out_specs=(
            P(("dp", "row"), "col"),
            P(("dp", "row"), "col"),
            P(None, "col"),
            P(None, "col"),
            P(None, "col"),
            P("col", "row"),
            P("col", "row"),
            P("col", "row"),
            P(None, "col", "row"),
            P(None, "col", "row"),
            P(None, "col", "row"),
            P("row", "col"),
            P("row", "col"),
            P("row", "col"),
            P("dp", "col", None, "row"),
            P("dp", "col", None, "row"),
            P("dp", "col", None, "row"),
            P("dp", "row", "col"),
            P("dp", "row", "col"),
            P("dp", "row", "col"),
        ),
        check_vma=False,
    )
```

```python
import jax
import jax.numpy as jnp
from jax import lax
from jax.sharding import PartitionSpec as P

MODEL_WIDTH = 1024
QUERY_HEADS = 16
KEY_VALUE_HEADS = 8
HEAD_SIZE = 64
FF = 512
EXPERTS = 32
TOP = 8
STEP = 10


norm_epsilon = 1e-06
first_decay = 0.9
second_decay = 0.95
adam_epsilon = 1e-08
weight_decay = 0.1
masked_score = -1e30
grid_axes = ("row", "col")
query_block = 384


def low(value):
    return value.astype(jnp.bfloat16)


def product(formula, left, right):
    return jnp.einsum(formula, left, right, preferred_element_type=jnp.float32)


def grid_split(rows):
    row_count, col_count = lax.axis_size("row"), lax.axis_size("col")
    tokens, width = rows.shape
    blocks = rows.reshape(row_count, tokens // row_count, col_count, width // col_count)
    return blocks.transpose(0, 2, 1, 3).reshape(
        row_count * col_count, tokens // row_count, width // col_count
    )


def copies(block, axes):
    count = 1
    for axis in axes:
        count *= lax.axis_size(axis)
    equal = jnp.broadcast_to(block[None], (count, *block.shape))
    return lax.all_to_all(equal, axes, split_axis=0, concat_axis=0, tiled=True)


def grid_whole(block, gather):
    row_count, col_count = lax.axis_size("row"), lax.axis_size("col")
    tokens, width = block.shape
    blocks = gather(block)
    blocks = blocks.reshape(row_count, col_count, tokens, width).transpose(0, 2, 1, 3)
    return blocks.reshape(row_count * tokens, col_count * width)


def grid_exchange(blocks):
    return lax.all_to_all(blocks, grid_axes, split_axis=0, concat_axis=0, tiled=True)


def col_exchange(blocks):
    return lax.all_to_all(blocks, "col", split_axis=0, concat_axis=0, tiled=True)


def gathered(block):
    return lax.all_gather(block, grid_axes, axis=0, tiled=False)


def copied(block):
    return copies(block, grid_axes)


def grid_total(blocks):
    return lax.psum_scatter(blocks, grid_axes, scatter_dimension=0, tiled=True)


def own_rows(value_rows, index, count):
    return lax.dynamic_slice_in_dim(value_rows, index * count, count, axis=0)


def whole_experts(blocks):
    grid = lax.axis_size("row") * lax.axis_size("col")
    if blocks.shape[0] % grid == 0:
        split = blocks.reshape(-1, grid, *blocks.shape[1:]).swapaxes(0, 1)
        return grid_exchange(split).swapaxes(0, 1), True
    every = lax.all_gather(blocks, "dp", axis=0, tiled=True)
    split = every.reshape(-1, grid, *every.shape[1:]).swapaxes(0, 1)
    return grid_exchange(split).swapaxes(0, 1), False


def expert_blocks(grads, experts_here, reduced):
    grid = grads.shape[1]
    if experts_here % grid == 0:
        if reduced:
            mine = lax.psum_scatter(grads, "dp", scatter_dimension=0, tiled=True)
        else:
            parts = lax.all_to_all(grads, "dp", split_axis=0, concat_axis=0, tiled=True)
            parts = parts.reshape(lax.axis_size("dp"), -1, *grads.shape[1:])
            mine = low(jnp.sum(parts.astype(jnp.float32), axis=0))
        mine = grid_exchange(mine.swapaxes(0, 1)).swapaxes(0, 1)
        return mine.reshape(experts_here, *grads.shape[2:])
    every = grid_exchange(grads.swapaxes(0, 1)).swapaxes(0, 1)
    every = every.reshape(-1, *grads.shape[2:])
    return lax.psum_scatter(every, "dp", scatter_dimension=0, tiled=True)


def attend(query_rows, key_rows, value_rows, allowed_blocks, scale_factor):
    contexts, totals = [], []
    tokens = key_rows.shape[0]
    for start in range(0, tokens, query_block):
        stop = start + query_block
        scores = product("gqd,td->gqt", query_rows[:, start:stop], key_rows[:stop]) * scale_factor
        scores = jnp.where(allowed_blocks[start // query_block], scores, masked_score)
        row_max = jnp.max(scores, axis=-1, keepdims=True)
        log_total = row_max + jnp.log(jnp.sum(jnp.exp(scores - row_max), axis=-1, keepdims=True))
        prob_low = low(jnp.exp(scores - log_total))
        contexts.append(low(product("gqt,td->gqd", prob_low, value_rows[:stop])))
        totals.append(log_total)
    return jnp.concatenate(contexts, axis=1), totals


def attend_back(query_rows, key_rows, value_rows, grad_rows, totals, allowed_blocks, scale_factor):
    tokens = key_rows.shape[0]
    grad_queries = []
    grad_keys = jnp.zeros(key_rows.shape, jnp.float32)
    grad_values = jnp.zeros(key_rows.shape, jnp.float32)
    for start in range(0, tokens, query_block):
        stop = start + query_block
        block_query = query_rows[:, start:stop]
        block_grad = grad_rows[:, start:stop]
        scores = product("gqd,td->gqt", block_query, key_rows[:stop]) * scale_factor
        scores = jnp.where(allowed_blocks[start // query_block], scores, masked_score)
        full = jnp.exp(scores - totals[start // query_block])
        grad_prob = product("gqd,td->gqt", block_grad, value_rows[:stop])
        inner = jnp.sum(full * grad_prob, axis=-1, keepdims=True)
        grad_scores = low(full * (grad_prob - inner))
        grad_queries.append(product("gqt,td->gqd", grad_scores, key_rows[:stop]) * scale_factor)
        rest = ((0, tokens - stop), (0, 0))
        grad_keys = grad_keys + jnp.pad(product("gqt,gqd->td", grad_scores, block_query), rest)
        grad_values = grad_values + jnp.pad(product("gqt,gqd->td", low(full), block_grad), rest)
    return jnp.concatenate(grad_queries, axis=1), grad_keys * scale_factor, grad_values


def adam_update(weight, moment, second, gradient, step_rate, decay_rate):
    moment_new = first_decay * moment + (1.0 - first_decay) * gradient
    second_new = second_decay * second + (1.0 - second_decay) * gradient * gradient
    step_size = step_rate / (1.0 - first_decay**STEP)
    denominator = jnp.sqrt(second_new / (1.0 - second_decay**STEP)) + adam_epsilon
    weight_new = weight - step_size * moment_new / denominator - step_rate * decay_rate * weight
    return (moment_new, second_new, weight_new)


def per_device(
    inputs,
    cotangent,
    routes,
    gate_probs,
    seq_ids,
    norm_gains,
    gain_moment,
    gain_second,
    query_weight,
    query_moment,
    query_second,
    key_value_matrix,
    key_value_first_moment,
    key_value_second_moment,
    out_weight,
    out_moment,
    out_second,
    gate_up_weight,
    gate_up_moment,
    gate_up_second,
    down_weight,
    down_moment,
    down_second,
):
    rep_tokens = routes.shape[0]
    row_count, col_count = lax.axis_size("row"), lax.axis_size("col")
    grid = row_count * col_count
    row_index, col_index = lax.axis_index("row"), lax.axis_index("col")
    place = row_index * col_count + col_index
    width_part = inputs.shape[1]
    key_width = key_value_matrix.shape[2]
    group_width = QUERY_HEADS // KEY_VALUE_HEADS
    head_span = group_width * HEAD_SIZE
    scale_factor = HEAD_SIZE ** (-0.5)
    capacity = rep_tokens * TOP // EXPERTS * 5 // 4
    own_count = EXPERTS // grid
    part_tokens = rep_tokens // grid
    half_tokens = rep_tokens // row_count
    ff_part = down_weight.shape[1]
    experts_here = gate_up_weight.shape[0]
    heads_here = key_width // HEAD_SIZE
    weight_in_here = low(
        jnp.concatenate(
            [
                query_weight.reshape(width_part, heads_here, head_span),
                key_value_matrix[0].reshape(width_part, heads_here, HEAD_SIZE),
                key_value_matrix[1].reshape(width_part, heads_here, HEAD_SIZE),
            ],
            axis=2,
        )
    ).transpose(1, 0, 2)
    head_width = weight_in_here.shape[2]
    inputs_all = grid_whole(inputs, gathered)
    weight_in = col_exchange(weight_in_here).reshape(MODEL_WIDTH, head_width)
    out_all = grid_whole(low(out_weight), copied)
    expert_weights = low(
        jnp.concatenate(
            [gate_up_weight.reshape(experts_here, width_part, 2 * ff_part), down_weight], axis=2
        )
    )
    expert_weights, spread = whole_experts(expert_weights)
    gate_up_mine = (
        expert_weights[..., : 2 * ff_part]
        .reshape(-1, row_count, col_count * width_part, 2 * ff_part)
        .transpose(0, 2, 1, 3)
        .reshape(-1, MODEL_WIDTH, 2 * FF)
    )
    down_mine = (
        expert_weights[..., 2 * ff_part :]
        .reshape(-1, row_count, col_count, ff_part, width_part)
        .transpose(0, 1, 3, 2, 4)
        .reshape(-1, FF, MODEL_WIDTH)
    )
    inputs_all, gate_up_mine = lax.optimization_barrier((inputs_all, gate_up_mine))
    if spread:
        gate_up_mine = lax.all_gather(gate_up_mine, "dp", axis=0, tiled=True)
        down_mine = lax.all_gather(down_mine, "dp", axis=0, tiled=True)
    cotangent_all = grid_whole(cotangent, gathered)
    gains_all = copies(norm_gains, ("col",)).transpose(1, 0, 2).reshape(2, MODEL_WIDTH)

    own_ids = jnp.arange(own_count, dtype=jnp.int32) * grid + place
    named = routes[:, :, None] == own_ids[None, None, :]
    token_weights = jnp.sum(jnp.where(named, gate_probs[:, :, None], 0.0), axis=1)
    chosen = jnp.any(named, axis=1)
    positions = jnp.arange(rep_tokens, dtype=jnp.int32)
    earlier = low(positions[:, None] > positions[None, :])
    slot_of = product("ts,si->it", earlier, low(chosen)).astype(jnp.int32)
    slot_of = jnp.where(chosen.T, slot_of, -1)
    slots = jnp.arange(capacity, dtype=jnp.int32)
    filled = slot_of[:, None, :] == slots[None, :, None]
    slot_weights = jnp.sum(jnp.where(filled, token_weights.T[:, None, :], 0.0), axis=2)[..., None]
    pick = low(filled)

    residual = inputs_all.astype(jnp.float32)
    first_scale = lax.rsqrt(jnp.mean(residual * residual, axis=1, keepdims=True) + norm_epsilon)
    normed = low(residual * first_scale * gains_all[0])
    projected = low(product("td,df->tf", normed, weight_in))
    query_rows = projected[:, :head_span].reshape(rep_tokens, group_width, HEAD_SIZE)
    query_rows = query_rows.transpose(1, 0, 2)
    key_rows = projected[:, head_span : head_span + HEAD_SIZE]
    value_rows = projected[:, head_span + HEAD_SIZE :]
    allowed_blocks = [
        (seq_ids[start : start + query_block, None] == seq_ids[None, : start + query_block])
        & (
            positions[None, : start + query_block]
            <= positions[start : start + query_block, None]
        )
        for start in range(0, rep_tokens, query_block)
    ]
    context, totals = attend(query_rows, key_rows, value_rows, allowed_blocks, scale_factor)
    context = context.transpose(1, 0, 2).reshape(rep_tokens, head_span)
    context_all = lax.all_gather(context, grid_axes, axis=1, tiled=True)
    middle = residual + product("th,hd->td", context_all, out_all)
    second_scale = lax.rsqrt(jnp.mean(middle * middle, axis=1, keepdims=True) + norm_epsilon)
    normed_two = low(middle * second_scale * gains_all[1])

    slot_inputs = low(product("ist,td->isd", pick, normed_two))
    weight_in_here, slot_inputs = lax.optimization_barrier((weight_in_here, slot_inputs))
    weight_in_all = lax.all_gather(weight_in_here, grid_axes, axis=0, tiled=False)
    weight_in_all = (
        weight_in_all.reshape(row_count, col_count, heads_here, width_part, head_width)
        .transpose(0, 2, 1, 3, 4)
        .reshape(grid, MODEL_WIDTH, head_width)
    )
    gate_up = product("isd,idf->isf", slot_inputs, gate_up_mine)
    gate_part = jnp.concatenate(
        [gate_up[..., 2 * r * ff_part : (2 * r + 1) * ff_part] for r in range(row_count)], axis=2
    )
    up_part = jnp.concatenate(
        [gate_up[..., (2 * r + 1) * ff_part : (2 * r + 2) * ff_part] for r in range(row_count)],
        axis=2,
    )
    hidden = low(jax.nn.silu(gate_part) * up_part)
    expert_out = low(product("isf,ifd->isd", hidden, down_mine) * slot_weights)
    mixture = low(product("ist,isd->td", pick, expert_out))
    mixture = grid_split(mixture).reshape(-1, width_part)

    grad_slots = low(product("ist,td->isd", pick, cotangent_all) * slot_weights)
    grad_hidden = product("isd,ifd->isf", grad_slots, down_mine)
    sigmoid_gate = jax.nn.sigmoid(gate_part)
    grad_gate = grad_hidden * up_part * sigmoid_gate * (1.0 + gate_part * (1.0 - sigmoid_gate))
    grad_up = grad_hidden * gate_part * sigmoid_gate
    grad_pair = low(
        jnp.concatenate(
            [
                side[..., r * ff_part : (r + 1) * ff_part]
                for r in range(row_count)
                for side in (grad_gate, grad_up)
            ],
            axis=2,
        )
    )
    back_slots = low(product("isf,idf->isd", grad_pair, gate_up_mine))
    grad_normed_two = low(product("ist,isd->td", pick, back_slots))
    grad_normed_two = grid_total(grad_normed_two).astype(jnp.float32)
    down_grads = low(product("isf,isd->ifd", hidden, grad_slots))
    gate_up_grads = low(product("isd,isf->idf", slot_inputs, grad_pair))
    gate_up_grads = gate_up_grads.reshape(
        own_count, col_count, width_part, row_count, 2 * ff_part
    ).transpose(0, 3, 1, 2, 4)
    gate_up_grads = gate_up_grads.reshape(own_count, grid, width_part, 2 * ff_part)
    down_grads = down_grads.reshape(
        own_count, row_count, ff_part, col_count, width_part
    ).transpose(0, 1, 3, 2, 4)
    down_grads = down_grads.reshape(own_count, grid, ff_part, width_part)
    grad_down = expert_blocks(down_grads, experts_here, False).astype(jnp.float32)

    middle_part = own_rows(middle, place, part_tokens)
    scale_part = own_rows(second_scale, place, part_tokens)
    inner = jnp.sum(grad_normed_two * gains_all[1] * middle_part, axis=1, keepdims=True)
    grad_middle = (
        own_rows(cotangent_all, place, part_tokens).astype(jnp.float32)
        + scale_part * gains_all[1] * grad_normed_two
        - middle_part * scale_part**3 * inner / MODEL_WIDTH
    )
    grad_gain_two = jnp.sum(grad_normed_two * middle_part * scale_part, axis=0)
    grad_middle_all = lax.all_gather(low(grad_middle), grid_axes, axis=0, tiled=True)

    gate_up_grads, mixture, grad_middle_all = lax.optimization_barrier(
        (gate_up_grads, mixture, grad_middle_all)
    )
    grad_gate_up = expert_blocks(gate_up_grads, experts_here, True).astype(jnp.float32)
    grad_gate_up = grad_gate_up.reshape(gate_up_weight.shape)
    mixture = grid_total(mixture).astype(jnp.float32)
    middle_here = lax.dynamic_slice(
        middle, (row_index * half_tokens, col_index * width_part), (half_tokens, width_part)
    )
    block_output = low(middle_here + mixture)

    out_mine = own_rows(out_all, place, head_span)
    grad_context = low(product("td,hd->th", grad_middle_all, out_mine))
    out_grads = product("th,td->hd", context, grad_middle_all)
    grad_context = grad_context.reshape(rep_tokens, group_width, HEAD_SIZE).transpose(1, 0, 2)
    grad_queries, grad_keys, grad_values = attend_back(
        query_rows, key_rows, value_rows, grad_context, totals, allowed_blocks, scale_factor
    )
    grad_queries = grad_queries.transpose(1, 0, 2).reshape(rep_tokens, head_span)
    grad_in = low(jnp.concatenate([grad_queries, grad_keys, grad_values], axis=1))
    grad_in_part = grid_exchange(grad_in.reshape(grid, part_tokens, head_width))
    weight_in_grads = product("td,tf->df", normed, grad_in)
    grad_normed = product("htf,hdf->td", grad_in_part, weight_in_all)

    residual_part = own_rows(residual, place, part_tokens)
    scale_part = own_rows(first_scale, place, part_tokens)
    inner = jnp.sum(grad_normed * gains_all[0] * residual_part, axis=1, keepdims=True)
    input_grad = (
        grad_middle
        + scale_part * gains_all[0] * grad_normed
        - residual_part * scale_part**3 * inner / MODEL_WIDTH
    )
    grad_gain_one = jnp.sum(grad_normed * residual_part * scale_part, axis=0)
    input_grad = input_grad.reshape(part_tokens, col_count, width_part).transpose(1, 0, 2)
    input_grad = col_exchange(input_grad).reshape(half_tokens, width_part)
    gain_grad = jnp.stack([grad_gain_one, grad_gain_two]).reshape(2, col_count, width_part)
    gain_grad = jnp.broadcast_to(
        gain_grad.transpose(1, 0, 2), (lax.axis_size("dp") * row_count, col_count, 2, width_part)
    )
    gain_grad = lax.all_to_all(
        gain_grad.reshape(-1, 2, width_part),
        ("dp", "row", "col"),
        split_axis=0,
        concat_axis=0,
        tiled=True,
    )
    gain_grad = jnp.sum(gain_grad, axis=0)

    head_blocks = jnp.concatenate(
        [
            low(weight_in_grads).reshape(col_count, width_part, head_width),
            low(out_grads)
            .reshape(head_span, col_count, width_part)
            .transpose(1, 2, 0),
        ],
        axis=2,
    )
    head_blocks = col_exchange(head_blocks)
    if lax.axis_size("dp") <= 4:
        head_blocks = jnp.sum(copies(head_blocks, ("dp",)).astype(jnp.float32), axis=0)
    else:
        head_blocks = lax.psum(head_blocks, "dp").astype(jnp.float32)
    query_grad = head_blocks[..., :head_span].transpose(1, 0, 2).reshape(query_weight.shape)
    key_value_grad = jnp.stack(
        [
            head_blocks[..., head_span : head_span + HEAD_SIZE],
            head_blocks[..., head_span + HEAD_SIZE : head_width],
        ]
    ).transpose(0, 2, 1, 3)
    key_value_grad = key_value_grad.reshape(key_value_matrix.shape)
    out_grad = head_blocks[..., head_width:].transpose(0, 2, 1).reshape(out_weight.shape)
    matrix_rate = 1.5 * MODEL_WIDTH ** (-0.5)
    gains_moment_new, gains_second_new, gains_new = adam_update(
        norm_gains, gain_moment, gain_second, gain_grad, 0.5, 0.0
    )
    query_moment_new, query_second_new, query_new = adam_update(
        query_weight, query_moment, query_second, query_grad, matrix_rate, weight_decay
    )
    pair_moment_new, pair_second_new, pair_new = adam_update(
        key_value_matrix,
        key_value_first_moment,
        key_value_second_moment,
        key_value_grad,
        matrix_rate,
        weight_decay,
    )
    out_moment_new, out_second_new, out_new = adam_update(
        out_weight,
        out_moment,
        out_second,
        out_grad,
        1.5 * max(1, QUERY_HEADS * HEAD_SIZE // 256) ** (-0.5),
        weight_decay,
    )
    gate_moment_new, gate_second_new, gate_new = adam_update(
        gate_up_weight, gate_up_moment, gate_up_second, grad_gate_up, matrix_rate, weight_decay
    )
    down_moment_new, down_second_new, down_new = adam_update(
        down_weight, down_moment, down_second, grad_down, 1.5 * (FF // 16) ** (-0.5), weight_decay
    )
    return (
        block_output,
        input_grad,
        gains_moment_new,
        gains_second_new,
        gains_new,
        query_moment_new,
        query_second_new,
        query_new,
        pair_moment_new,
        pair_second_new,
        pair_new,
        out_moment_new,
        out_second_new,
        out_new,
        gate_moment_new,
        gate_second_new,
        gate_new,
        down_moment_new,
        down_second_new,
        down_new,
    )


def solution(mesh):
    return jax.shard_map(
        per_device,
        mesh=mesh,
        in_specs=(
            P(("dp", "row"), "col"),
            P(("dp", "row"), "col"),
            P("dp", None),
            P("dp", None),
            P("dp"),
            P(None, "col"),
            P(None, "col"),
            P(None, "col"),
            P("col", "row"),
            P("col", "row"),
            P("col", "row"),
            P(None, "col", "row"),
            P(None, "col", "row"),
            P(None, "col", "row"),
            P("row", "col"),
            P("row", "col"),
            P("row", "col"),
            P("dp", "col", None, "row"),
            P("dp", "col", None, "row"),
            P("dp", "col", None, "row"),
            P("dp", "row", "col"),
            P("dp", "row", "col"),
            P("dp", "row", "col"),
        ),
        out_specs=(
            P(("dp", "row"), "col"),
            P(("dp", "row"), "col"),
            P(None, "col"),
            P(None, "col"),
            P(None, "col"),
            P("col", "row"),
            P("col", "row"),
            P("col", "row"),
            P(None, "col", "row"),
            P(None, "col", "row"),
            P(None, "col", "row"),
            P("row", "col"),
            P("row", "col"),
            P("row", "col"),
            P("dp", "col", None, "row"),
            P("dp", "col", None, "row"),
            P("dp", "col", None, "row"),
            P("dp", "row", "col"),
            P("dp", "row", "col"),
            P("dp", "row", "col"),
        ),
        check_vma=False,
    )
```
